128 devices in a mesh: pipe: 2 (over x_lo), patch: 32 (over z, y, core), head: 2 (over x_hi).
Axes of the slice: x: 4 (x_hi: 2, x_lo: 2; x = x_hi * 2 + x_lo), y: 4, z: 4, core: 2. Of those that a mesh axis runs over, the one named last changes fastest.
Arguments:
- queries: bfloat16 [2, 6144, 2560], P('pipe', ('patch', 'head')), may hold values from -40 to 40
- fresh_keys: bfloat16 [2, 6144, 2560], P('pipe', ('patch', 'head')), may hold values from -6 to 6
- fresh_values: bfloat16 [2, 6144, 2560], P('pipe', ('patch', 'head')), may hold values from -6 to 6
- stale_keys: bfloat16 [2, 6144, 2560], P('pipe', 'patch', 'head'), may hold values from -40 to 40
- stale_values: bfloat16 [2, 6144, 2560], P('pipe', 'patch', 'head'), may hold values from -6 to 6
- out_weight: bfloat16 [2, 2560, 5120], P('pipe', 'head'), may hold values from -0.5 to 0.5
- out_gate: float32 [2, 5120], P('pipe'), may hold values from 0.5 to 2
Outputs:
- new_keys: bfloat16 [2, 6144, 2560], P('pipe', 'patch', 'head')
- new_values: bfloat16 [2, 6144, 2560], P('pipe', 'patch', 'head')
- onward: bfloat16 [2, 6144, 5120], P('pipe', ('patch', 'head'))
The draws below stay inside these ranges and needn't reach their ends.
All inputs are finite; a program needn't handle non-finite values.
Results may differ from the reference program's by a relative error of at most 0.014.
Values may be sent and summed in bfloat16 or wider, within the bound.
No kernel may reach another device: no remote copies, remote signals or barrier semaphores. Data moves between devices by JAX's collectives and lax.ppermute only.
A program may use at most 192 MiB of HBM per device.

```python
import math
import jax
import jax.numpy as jnp
from jax import lax

D = 5120
HEADS = 20
HEAD_DIM = 128
SECTIONS = 2
LENGTH = 6144
N_PATCH = 32
N_HEAD = 2


def draw_queries(key, part):
    key = jax.random.fold_in(key, 11)
    first_key = jax.random.fold_in(key, 0)
    full_shape = (SECTIONS, LENGTH, HEADS, HEAD_DIM)
    sample = 2.0 * jax.random.normal(first_key, full_shape, jnp.float32)
    sample = jnp.clip(sample, -40.0, 40.0)
    return sample.reshape(SECTIONS, LENGTH, HEADS * HEAD_DIM).astype(jnp.bfloat16)


def draw_stale_keys(key, part):
    key = jax.random.fold_in(key, 23)
    first_key = jax.random.fold_in(key, 0)
    full_shape = (SECTIONS, LENGTH, HEADS, HEAD_DIM)
    sample = jax.random.normal(first_key, full_shape, jnp.float32)
    sample = jnp.clip(sample, -40.0, 40.0)
    return sample.reshape(SECTIONS, LENGTH, HEADS * HEAD_DIM).astype(jnp.bfloat16)


def level_of(own_key, extent, shards, least, top_value):
    factor_of = 1.0
    for position, parts in shards:
        steps = jax.random.uniform(jax.random.fold_in(jax.random.fold_in(own_key, 6), position), (parts,), jnp.float32, least / len(shards), top_value / len(shards))
        factor_of = factor_of * jnp.repeat(jnp.exp(steps), extent[position] // parts).reshape((-1,) + (1,) * (len(extent) - 1 - position))
    return factor_of


def bell_draw(key, extent, scale, reach, pieces=(), kind=jnp.bfloat16):
    level = level_of(key, extent, pieces, -0.22, 0.18) if pieces else 1.0
    values = jax.random.normal(key, extent, jnp.float32) * scale * level
    return jnp.minimum(jnp.maximum(values, -reach), reach).astype(kind)


def setup_inputs(seed: int = 0) -> dict:
    keys = jax.random.split(jax.random.key(seed), 8)
    return {
        "queries": draw_queries(jax.random.fold_in(keys[7], 71), 0),
        "fresh_keys": bell_draw(keys[1], (SECTIONS, LENGTH, HEADS * HEAD_DIM), 1.0, 6.0, ((0, 2), (1, 64))),
        "fresh_values": bell_draw(keys[2], (SECTIONS, LENGTH, HEADS * HEAD_DIM), 1.0, 6.0, ((0, 2), (1, 64))),
        "stale_keys": draw_stale_keys(jax.random.fold_in(keys[7], 71), 0),
        "stale_values": bell_draw(keys[4], (SECTIONS, LENGTH, HEADS * HEAD_DIM), 1.0, 6.0, ((0, 2), (1, 32), (2, 2))),
        "out_weight": bell_draw(keys[5], (SECTIONS, HEADS * HEAD_DIM, D), HEAD_DIM ** -0.5, 0.5, ((0, 2), (1, 2))),
        "out_gate": jnp.clip(jnp.exp(math.log(2.0) - 1.3862944 * jax.random.uniform(keys[6], (SECTIONS, D), jnp.float32) ** level_of(keys[6], (SECTIONS, D), ((0, 2),), -0.2, 0.2)), 0.5, 2.0),
    }


def section(queries, fresh_keys, fresh_values, stale_keys, stale_values, out_weight, out_gate):
    patch_rows = LENGTH // N_PATCH
    score_scale = HEAD_DIM ** -0.5
    group_width = HEADS * HEAD_DIM // N_HEAD

    def one_patch(patch_index):
        first_row = (patch_index * patch_rows).astype(jnp.int32)
        query_rows = lax.dynamic_slice_in_dim(queries, first_row, patch_rows, 0)
        own_keys = lax.dynamic_slice_in_dim(fresh_keys, first_row, patch_rows, 0)
        own_values = lax.dynamic_slice_in_dim(fresh_values, first_row, patch_rows, 0)
        keys_used = lax.dynamic_update_slice_in_dim(stale_keys, own_keys, first_row, 0)
        values_used = lax.dynamic_update_slice_in_dim(stale_values, own_values, first_row, 0)
        query_heads = query_rows.astype(jnp.float32).reshape(patch_rows, HEADS, HEAD_DIM)
        key_heads = keys_used.astype(jnp.float32).reshape(LENGTH, HEADS, HEAD_DIM)
        value_heads = values_used.astype(jnp.float32).reshape(LENGTH, HEADS, HEAD_DIM)
        scores = jnp.einsum("qhd,khd->hqk", query_heads, key_heads) * score_scale
        row_top = jnp.max(scores, axis=-1, keepdims=True)
        weights = jnp.exp(scores - row_top)
        row_total = jnp.sum(weights, axis=-1)
        rounded = lax.optimization_barrier(weights.astype(jnp.bfloat16)).astype(jnp.float32)
        numerator = jnp.einsum("hqk,khd->qhd", rounded, value_heads)
        attended = (numerator / jnp.transpose(row_total)[:, :, None]).reshape(patch_rows, HEADS * HEAD_DIM)
        attended = attended.astype(jnp.bfloat16)
        summed = jnp.zeros((patch_rows, D), jnp.float32)
        for group in range(N_HEAD):
            lower = group * group_width
            partial_value = jnp.dot(attended[:, lower:lower + group_width], out_weight[lower:lower + group_width], preferred_element_type=jnp.float32)
            partial_value = lax.optimization_barrier(partial_value.astype(jnp.bfloat16)).astype(jnp.float32)
            summed = summed + partial_value
        return (summed * out_gate[None, :]).astype(jnp.bfloat16)

    blocks = lax.map(one_patch, jnp.arange(N_PATCH, dtype=jnp.int32))
    return blocks.reshape(LENGTH, D)


def reference(queries, fresh_keys, fresh_values, stale_keys, stale_values, out_weight, out_gate):
    results = []
    for layer in range(SECTIONS):
        results.append(section(queries[layer], fresh_keys[layer], fresh_values[layer], stale_keys[layer], stale_values[layer], out_weight[layer], out_gate[layer]))
    stacked = jnp.stack(results, axis=0)
    onward = jnp.roll(stacked, 1, axis=0)
    return (fresh_keys, fresh_values, onward)
```

```python
import functools
import math
import jax
import jax.numpy as jnp
from jax import lax
from jax.experimental import pallas as pl
from jax.experimental.pallas import tpu as pltpu
from jax.sharding import PartitionSpec as P

HEAD_DIM = 128
CHIPS = 4
SCALE_LOG2 = HEAD_DIM ** (-0.5) / math.log(2.0)
BF = jnp.bfloat16
F32 = jnp.float32
VMEM_LIMIT = 40 * 1024 * 1024


def place(z, y, core):
    return ((z % CHIPS) * CHIPS + y % CHIPS) * 2 + core


def along(value, steps, core_on_y):
    pairs = []
    for z in range(CHIPS):
        for y in range(CHIPS):
            for core in range(2):
                to = place(z, y + steps, core) if core == core_on_y else place(z + steps, y, core)
                pairs.append((place(z, y, core), to))
    return lax.ppermute(value, "patch", pairs)


def keys_along(value, steps):
    return along(value, steps, 0)


def queries_along(value, steps):
    return along(value, steps, 1)


def other_core(value):
    return lax.ppermute(value, "patch", [(i, i ^ 1) for i in range(2 * CHIPS * CHIPS)])


def other_half(value, core, head):
    pairs = [
        (b * 2 + h, (b ^ core) * 2 + (h ^ head)) for b in range(2 * CHIPS * CHIPS) for h in range(2)
    ]
    return lax.ppermute(value, ("patch", "head"), pairs)


def onward_to(value, head):
    pairs = [(p * 2 + h, (1 - p) * 2 + (h ^ head)) for p in range(2) for h in range(2)]
    return lax.ppermute(value, ("pipe", "head"), pairs)


def params(**kw):
    return pltpu.CompilerParams(vmem_limit_bytes=VMEM_LIMIT, **kw)


def cost(flops, nbytes, trans=0):
    return pl.CostEstimate(flops=flops, bytes_accessed=nbytes, transcendentals=trans)


def column_blocks(arrays, places, width):
    rows = [arrays[a].shape[0] for a, _ in places]
    table = jnp.stack([jnp.asarray(p, jnp.int32) for _, p in places])
    n = len(places)

    def body(table_ref, *refs):
        for i in range(n):
            refs[n + i][...] = refs[i][...]

    return pl.pallas_call(
        body,
        grid_spec=pltpu.PrefetchScalarGridSpec(
            num_scalar_prefetch=1,
            grid=(1,),
            in_specs=[
                pl.BlockSpec((rows[i], width), functools.partial(lambda i, g, t: (0, t[i]), i))
                for i in range(n)
            ],
            out_specs=[pl.BlockSpec((rows[i], width), lambda g, t: (0, 0)) for i in range(n)],
        ),
        out_shape=[jax.ShapeDtypeStruct((rows[i], width), arrays[0].dtype) for i in range(n)],
        compiler_params=params(),
    )(table, *[arrays[a] for a, _ in places])


def nt(a, b):
    return lax.dot_general(a, b, (((1,), (1,)), ((), ())), preferred_element_type=F32)


def scores_max(pieces):
    by_width = {}
    for s in pieces:
        w = s.shape[1]
        by_width[w] = s if w not in by_width else jnp.maximum(by_width[w], s)
    top = None
    for s in by_width.values():
        t = jnp.max(s, axis=1, keepdims=True)
        top = t if top is None else jnp.maximum(top, t)
    return top


def attend(q, keys, values, state):
    pieces = [nt(q, k) for k in keys]
    top = scores_max(pieces)
    if state is not None:
        top = jnp.maximum(top, state[0])
    sums = None
    for s, v in zip(pieces, values):
        w = jnp.exp2((s - top) * SCALE_LOG2).astype(BF)
        ones = jnp.ones(v.shape, BF)
        part = jnp.dot(w, jnp.concatenate([v, ones], axis=1), preferred_element_type=F32)
        sums = part if sums is None else sums + part
    total = sums[:, HEAD_DIM : HEAD_DIM + 1]
    sums = sums[:, :HEAD_DIM]
    if state is not None:
        keep = jnp.exp2((state[0] - top) * SCALE_LOG2)
        total = total + keep * state[1]
        sums = sums + keep * state[2]
    return top, total, sums


def lane(x, shape):
    return lax.broadcasted_iota(jnp.int32, shape, 1) == x


def first_kernel(row_sets, n_keys, *refs):
    n_q = len(row_sets)
    q_refs = refs[:n_q]
    k_refs = refs[n_q : n_q + n_keys]
    v_refs = refs[n_q + n_keys : n_q + 2 * n_keys]
    s_refs = refs[n_q + 2 * n_keys : 2 * n_q + 2 * n_keys]
    t_refs = refs[2 * n_q + 2 * n_keys :]
    head = pl.program_id(0)
    for i in range(n_q):
        for lo, hi, use in row_sets[i]:
            ks = [k_refs[j][a:b, :] for j, a, b in use]
            vs = [v_refs[j][a:b, :] for j, a, b in use]
            top, total, sums = attend(q_refs[i][lo:hi, :], ks, vs, None)
            s_refs[i][lo:hi, :] = sums
            shape = (hi - lo, HEAD_DIM)
            old = jnp.where(head == 0, 0.0, t_refs[i][lo:hi, :])
            new = jnp.where(lane(head, shape), top, old)
            t_refs[i][lo:hi, :] = jnp.where(lane(head + 8, shape), total, new)


def first_part(queries, keys, values, row_sets):
    n_q, n_k = len(queries), len(keys)
    heads = queries[0].shape[1] // HEAD_DIM
    per_head = lambda a: pl.BlockSpec((a.shape[0], HEAD_DIM), lambda h: (0, h))
    whole = lambda a: pl.BlockSpec((a.shape[0], HEAD_DIM), lambda h: (0, 0))
    work = sum(
        (hi - lo) * sum(b - a for _, a, b in use) for rows in row_sets for lo, hi, use in rows
    )
    outs = pl.pallas_call(
        functools.partial(first_kernel, row_sets, n_k),
        grid=(heads,),
        in_specs=[per_head(a) for a in (*queries, *keys, *values)],
        out_specs=[per_head(a) for a in queries] + [whole(a) for a in queries],
        out_shape=[jax.ShapeDtypeStruct(a.shape, F32) for a in queries]
        + [jax.ShapeDtypeStruct((a.shape[0], HEAD_DIM), F32) for a in queries],
        compiler_params=params(),
        cost_estimate=cost(8 * work * heads * HEAD_DIM, 8 * 2**20, work * heads),
    )(*queries, *keys, *values)
    return outs[:n_q], outs[n_q:]


def last_kernel(n_q, *refs):
    q_refs, s_refs, t_refs = refs[:n_q], refs[n_q : 2 * n_q], refs[2 * n_q : 3 * n_q]
    k_ref, v_ref = refs[3 * n_q : 3 * n_q + 2]
    o_refs = refs[3 * n_q + 2 :]
    rows = k_ref.shape[0]
    heads = o_refs[0].shape[1] // HEAD_DIM - 1
    shape = (192, HEAD_DIM)
    for i in range(n_q):
        for lo in range(0, rows, 192):
            packed = jnp.zeros(shape, F32)
            for h in range(heads):
                cols = slice(h * HEAD_DIM, (h + 1) * HEAD_DIM)
                here = slice(lo, lo + 192)
                state = (t_refs[i][here, h : h + 1], t_refs[i][here, 8 + h : 9 + h], s_refs[i][here, cols])
                top, total, sums = attend(q_refs[i][here, cols], [k_ref[:, cols]], [v_ref[:, cols]], state)
                o_refs[i][here, cols] = (sums / total).astype(BF)
                level = top * SCALE_LOG2 + jnp.log2(total)
                for part in range(3):
                    piece = level.astype(BF).astype(F32)
                    packed = jnp.where(lane(3 * h + part, shape), piece, packed)
                    level = level - piece
            o_refs[i][lo : lo + 192, heads * HEAD_DIM :] = packed.astype(BF)


def last_part(queries, sums, stats, key, value):
    n_q = len(queries)
    rows, width = queries[0].shape
    heads = width // HEAD_DIM
    whole = lambda a: pl.BlockSpec(a.shape, lambda: (0, 0))
    out = jax.ShapeDtypeStruct((rows, width + HEAD_DIM), BF)
    return pl.pallas_call(
        functools.partial(last_kernel, n_q),
        in_specs=[whole(a) for a in (*queries, *sums, *stats, key, value)],
        out_specs=[whole(out)] * n_q,
        out_shape=[out] * n_q,
        compiler_params=params(),
        cost_estimate=cost(8 * n_q * rows * rows * width, 4 * 2**20, n_q * rows * rows * heads),
    )(*queries, *sums, *stats, key, value)


def combine_kernel(a_ref, b_ref, c_ref, d_ref, same_ref, other_ref):
    refs = (a_ref, b_ref, c_ref, d_ref)
    heads = a_ref.shape[1] // HEAD_DIM - 1
    half = same_ref.shape[0]
    for lo, out in ((0, same_ref), (half, other_ref)):
        here = slice(lo, lo + half)
        for h in range(heads):
            cols = slice(h * HEAD_DIM, (h + 1) * HEAD_DIM)
            levels = []
            for r in refs:
                at = heads * HEAD_DIM + 3 * h
                s = r[here, at : at + 3].astype(F32)
                levels.append(s[:, 0:1] + s[:, 1:2] + s[:, 2:3])
            top = functools.reduce(jnp.maximum, levels)
            shares = [jnp.exp2(x - top) for x in levels]
            total = shares[0] + shares[1] + shares[2] + shares[3]
            acc = None
            for r, w in zip(refs, shares):
                part = r[here, cols].astype(F32) * (w / total)
                acc = part if acc is None else acc + part
            out[:, cols] = acc.astype(BF)


def combine(parts):
    rows, width = parts[0].shape
    out = jax.ShapeDtypeStruct((rows // 2, width - HEAD_DIM), BF)
    return pl.pallas_call(
        combine_kernel,
        out_shape=[out, out],
        compiler_params=params(),
        cost_estimate=cost(rows * width * 20, 4 * 2**20),
    )(*parts)


def project_kernel(core_ref, a_ref, b_ref, wa_ref, wb_ref, g_ref, first_ref, second_ref):
    half = first_ref.shape[0]
    r = jnp.dot(a_ref[...], wa_ref[...], preferred_element_type=F32)
    r += jnp.dot(b_ref[...], wb_ref[...], preferred_element_type=F32)
    r = (r * g_ref[...]).astype(BF)
    first_ref[...] = r[:half]
    second_ref[...] = r[half:]


def project(core, mine, theirs, weight, gate):
    rows, depth = mine.shape
    width = weight.shape[1]
    tile = 1024
    out = jax.ShapeDtypeStruct((rows // 2, width), BF)
    return pl.pallas_call(
        project_kernel,
        grid_spec=pltpu.PrefetchScalarGridSpec(
            num_scalar_prefetch=1,
            grid=(width // tile,),
            in_specs=[
                pl.BlockSpec((rows, depth), lambda j, c: (0, 0)),
                pl.BlockSpec((rows, depth), lambda j, c: (0, 0)),
                pl.BlockSpec((depth, tile), lambda j, c: (c[0], j)),
                pl.BlockSpec((depth, tile), lambda j, c: (1 - c[0], j)),
                pl.BlockSpec((1, tile), lambda j, c: (0, j)),
            ],
            out_specs=[pl.BlockSpec((rows // 2, tile), lambda j, c: (0, j))] * 2,
        ),
        out_shape=[out, out],
        compiler_params=params(),
        cost_estimate=cost(4 * rows * depth * width, weight.size * 2),
    )(core, mine, theirs, weight, weight, gate)


def per_device(queries, fresh_keys, fresh_values, stale_keys, stale_values, out_weight, out_gate):
    half = queries.shape[1]
    patch = 2 * half
    width = queries.shape[2] // 4
    head = lax.axis_index("head")
    core = lax.axis_index("patch") % 2
    core_table = jnp.reshape(core, (1,)).astype(jnp.int32)

    sk, sk_out, sv, sv_out = column_blocks(
        [stale_keys[0], stale_values[0]], [(0, core), (0, 1 - core), (1, core), (1, 1 - core)], width
    )
    q_mine, q_head, q_core, q_both = column_blocks(
        [queries[0]],
        [
            (0, head * 2 + core),
            (0, (1 - head) * 2 + core),
            (0, head * 2 + 1 - core),
            (0, (1 - head) * 2 + 1 - core),
        ],
        width,
    )
    q_head, q_core, q_both = (
        other_half(q_head, 0, 1),
        other_half(q_core, 1, 0),
        other_half(q_both, 1, 1),
    )
    k_own = jnp.concatenate([sk, other_core(sk_out)], axis=0)
    v_own = jnp.concatenate([sv, other_core(sv_out)], axis=0)
    q_own = jnp.concatenate([q_mine, q_head, q_core, q_both], axis=0)

    k_up, k_down = keys_along(k_own, 1), keys_along(k_own, -1)
    v_up, v_down = keys_along(v_own, 1), keys_along(v_own, -1)
    q_far = queries_along(q_own, 2)
    q_up, q_down = queries_along(q_own, 1), queries_along(q_own, -1)
    k_far = keys_along(k_up, 1)
    v_far = keys_along(v_down, -1)

    def exchanged(fresh):
        mine, out = column_blocks([fresh[0]], [(0, head), (0, 1 - head)], 2 * width)
        got = other_half(out, 0, 1)
        low, high = jnp.where(head == 0, mine, got), jnp.where(head == 0, got, mine)
        return jnp.concatenate([low, high], axis=0)

    new_keys, new_values = exchanged(fresh_keys), exchanged(fresh_values)
    fk, fk_out, fv, fv_out = column_blocks(
        [new_keys, new_values], [(0, core), (0, 1 - core), (1, core), (1, 1 - core)], width
    )
    fk_core, fv_core = other_core(fk_out), other_core(fv_out)

    every = [(0, 0, 2 * patch), (1, 0, 2 * patch), (2, 0, 2 * patch)]
    plain = [(0, patch, every), (patch, 2 * patch, every)]
    mixed = [
        (0, patch, [(3, 0, patch), (0, patch, 2 * patch), (1, 0, 2 * patch), (2, 0, 2 * patch)]),
        (patch, 2 * patch, [(4, 0, patch), (0, 0, patch), (1, 0, 2 * patch), (2, 0, 2 * patch)]),
    ]
    s_out, t_out = first_part(
        [q_far, q_up, q_down], [k_own, k_up, k_down], [v_own, v_up, v_down], [plain] * 3
    )
    s_own, t_own = first_part(
        [q_own], [k_own, k_up, k_down, fk, fk_core], [v_own, v_up, v_down, fv, fv_core], [mixed]
    )
    o_far, o_up, o_down = last_part([q_far, q_up, q_down], s_out, t_out, k_far, v_far)
    (o_own,) = last_part([q_own], s_own, t_own, k_far, v_far)
    parts = (o_own, queries_along(o_far, 2), queries_along(o_up, -1), queries_along(o_down, 1))
    mine, out = combine(parts)
    theirs = other_core(out)
    first, second = project(core_table, mine, theirs, out_weight[0], out_gate)
    first, second = onward_to(first, 0), onward_to(second, 1)
    branch = (first.astype(F32) + second.astype(F32)).astype(BF)
    return (new_keys[None], new_values[None], branch[None])


def solution(mesh):
    in_specs = (
        P("pipe", ("patch", "head"), None),
        P("pipe", ("patch", "head"), None),
        P("pipe", ("patch", "head"), None),
        P("pipe", "patch", "head"),
        P("pipe", "patch", "head"),
        P("pipe", "head", None),
        P("pipe", None),
    )
    out_specs = (
        P("pipe", "patch", "head"),
        P("pipe", "patch", "head"),
        P("pipe", ("patch", "head"), None),
    )
    return jax.shard_map(
        per_device, mesh=mesh, in_specs=in_specs, out_specs=out_specs, check_vma=False
    )
```

```python
import functools
import math
import jax
import jax.numpy as jnp
from jax import lax
from jax.experimental import pallas as pl
from jax.experimental.pallas import tpu as pltpu
from jax.sharding import PartitionSpec as P

HEAD_DIM = 128
CHIPS = 4
SCALE_LOG2 = HEAD_DIM ** (-0.5) / math.log(2.0)
BF = jnp.bfloat16
F32 = jnp.float32
VMEM_LIMIT = 20 * 1024 * 1024


def place(z, y, core):
    return ((z % CHIPS) * CHIPS + y % CHIPS) * 2 + core


def along(value, steps, core_on_y):
    pairs = []
    for z in range(CHIPS):
        for y in range(CHIPS):
            for core in range(2):
                to = place(z, y + steps, core) if core == core_on_y else place(z + steps, y, core)
                pairs.append((place(z, y, core), to))
    return lax.ppermute(value, "patch", pairs)


def keys_along(value, steps):
    return along(value, steps, 0)


def queries_along(value, steps):
    return along(value, steps, 1)


def other_core(value):
    return lax.ppermute(value, "patch", [(i, i ^ 1) for i in range(2 * CHIPS * CHIPS)])


def other_half(value, core, head):
    pairs = [
        (b * 2 + h, (b ^ core) * 2 + (h ^ head)) for b in range(2 * CHIPS * CHIPS) for h in range(2)
    ]
    return lax.ppermute(value, ("patch", "head"), pairs)


def onward_to(value, head):
    pairs = [(p * 2 + h, (1 - p) * 2 + (h ^ head)) for p in range(2) for h in range(2)]
    return lax.ppermute(value, ("pipe", "head"), pairs)


def params(limit=VMEM_LIMIT):
    return pltpu.CompilerParams(vmem_limit_bytes=limit)


def cost(flops, nbytes, trans=0):
    return pl.CostEstimate(flops=flops, bytes_accessed=nbytes, transcendentals=trans)


def split_by_core(table, keys, values, queries):
    rows, width = keys.shape[1], keys.shape[2] // 2
    few = queries.shape[1]

    def body(table_ref, k_ref, v_ref, q_ref, same_ref, q_same_ref, other_ref, sems):
        head, core = table_ref[0], table_ref[1]

        def columns(ref, i):
            return ref.at[0, :, pl.ds(pl.multiple_of(i * width, HEAD_DIM), width)]

        moves = [
            (columns(k_ref, 1 - core), other_ref.at[pl.ds(0, rows)]),
            (columns(v_ref, 1 - core), other_ref.at[pl.ds(rows, rows)]),
            (columns(q_ref, 2 * head + 1 - core), other_ref.at[pl.ds(2 * rows, few)]),
            (columns(q_ref, 2 * (1 - head) + 1 - core), other_ref.at[pl.ds(2 * rows + few, few)]),
            (columns(k_ref, core), same_ref.at[pl.ds(0, rows)]),
            (columns(v_ref, core), same_ref.at[pl.ds(rows, rows)]),
            (columns(q_ref, 2 * head + core), q_same_ref.at[pl.ds(0, few)]),
            (columns(q_ref, 2 * (1 - head) + core), q_same_ref.at[pl.ds(few, few)]),
        ]
        copies = [pltpu.make_async_copy(a, b, sems.at[i]) for i, (a, b) in enumerate(moves)]
        for c in copies:
            c.start()
        for c in copies:
            c.wait()

    vmem = pl.BlockSpec(memory_space=pltpu.VMEM)
    hbm = pl.BlockSpec(memory_space=pltpu.HBM)
    return pl.pallas_call(
        body,
        in_specs=[pl.BlockSpec(memory_space=pltpu.SMEM), hbm, hbm, hbm],
        out_specs=[vmem] * 3,
        out_shape=[
            jax.ShapeDtypeStruct((2 * rows, width), BF),
            jax.ShapeDtypeStruct((2 * few, width), BF),
            jax.ShapeDtypeStruct((2 * rows + 2 * few, width), BF),
        ],
        scratch_shapes=[pltpu.SemaphoreType.DMA((8,))],
        compiler_params=params(),
    )(table, keys, values, queries)


def outgoing_fresh(head, keys, values):
    rows, width = keys.shape[0], keys.shape[1] // 2

    def body(head_ref, k_ref, v_ref, out_ref):
        out_ref[:rows] = k_ref[...]
        out_ref[rows:] = v_ref[...]

    block = pl.BlockSpec((rows, width), lambda g, h: (0, 1 - h[0]))
    return pl.pallas_call(
        body,
        grid_spec=pltpu.PrefetchScalarGridSpec(
            num_scalar_prefetch=1,
            grid=(1,),
            in_specs=[block, block],
            out_specs=pl.BlockSpec((2 * rows, width), lambda g, h: (0, 0)),
        ),
        out_shape=jax.ShapeDtypeStruct((2 * rows, width), BF),
        compiler_params=params(),
    )(head, keys, values)


def assemble_fresh(table, keys, values, got):
    rows, width = keys.shape[0], keys.shape[1] // 2
    narrow = width // 2

    def body(table_ref, k_ref, v_ref, got_ref, nk_ref, nv_ref, same_ref, other_ref):
        head, core = table_ref[0], table_ref[1]
        for mine, at, new in ((k_ref, 0, nk_ref), (v_ref, rows, nv_ref)):
            theirs = got_ref[at : at + rows]
            low = jnp.where(head == 0, mine[...], theirs)
            high = jnp.where(head == 0, theirs, mine[...])
            new[:rows] = low
            new[rows:] = high
            for lo, x in ((2 * at, low), (2 * at + rows, high)):
                left, right = x[:, :narrow], x[:, narrow:]
                same_ref[lo : lo + rows] = jnp.where(core == 0, left, right)
                other_ref[lo : lo + rows] = jnp.where(core == 0, right, left)

    block = pl.BlockSpec((rows, width), lambda g, t: (0, t[0]))
    whole = lambda r, w: pl.BlockSpec((r, w), lambda g, t: (0, 0))
    return pl.pallas_call(
        body,
        grid_spec=pltpu.PrefetchScalarGridSpec(
            num_scalar_prefetch=1,
            grid=(1,),
            in_specs=[block, block, whole(2 * rows, width)],
            out_specs=[whole(2 * rows, width)] * 2 + [whole(4 * rows, narrow)] * 2,
        ),
        out_shape=[jax.ShapeDtypeStruct((2 * rows, width), BF)] * 2
        + [jax.ShapeDtypeStruct((4 * rows, narrow), BF)] * 2,
        compiler_params=params(),
    )(table, keys, values, got)


def nt(a, b):
    return lax.dot_general(a, b, (((1,), (1,)), ((), ())), preferred_element_type=F32)


def with_ones(v):
    return jnp.concatenate([v, jnp.ones(v.shape, BF)], axis=1)


def lanes(shape):
    return lax.broadcasted_iota(jnp.int32, shape, 1)


def attend(jobs, q_ref, o_ref):
    heads = q_ref.shape[1] // HEAD_DIM
    work = [(i, h) for h in range(heads) for i in range(len(jobs))]

    def columns(refs, h):
        cols = slice(h * HEAD_DIM, (h + 1) * HEAD_DIM)
        return jnp.concatenate([r[lo:hi, cols] for r, lo, hi in refs], axis=0)

    def product(i, h):
        here, keys, _ = jobs[i]
        return nt(q_ref[here, h * HEAD_DIM : (h + 1) * HEAD_DIM], columns(keys, h))

    shapes = [(here.stop - here.start, HEAD_DIM) for here, _, _ in jobs]
    tops = [jnp.zeros(s, F32) for s in shapes]
    totals = [jnp.ones(s, F32) for s in shapes]
    scores = product(*work[0])
    for n, (i, h) in enumerate(work):
        later = product(*work[n + 1]) if n + 1 < len(work) else None
        here, _, values = jobs[i]
        top = jnp.max(scores, axis=1, keepdims=True)
        w = jnp.exp2((scores - top) * SCALE_LOG2).astype(BF)
        part = jnp.dot(w, with_ones(columns(values, h)), preferred_element_type=F32)
        total = part[:, HEAD_DIM:]
        o_ref[here, h * HEAD_DIM : (h + 1) * HEAD_DIM] = (part[:, :HEAD_DIM] / total).astype(BF)
        at = lanes(shapes[i]) == h
        tops[i] = jnp.where(at, top, tops[i])
        totals[i] = jnp.where(at, total, totals[i])
        scores = later
    for (here, _, _), top, total in zip(jobs, tops, totals):
        level = top * SCALE_LOG2 + jnp.log2(total)
        high = level.astype(BF).astype(F32)
        rest = level - high
        middle = rest.astype(BF).astype(F32)
        packed = high + pltpu.roll(middle, 8, 1) + pltpu.roll(rest - middle, 16, 1)
        o_ref[here, heads * HEAD_DIM :] = packed.astype(BF)


def halves(refs):
    rows = refs[0].shape[0] // 2
    return [(r, 0, rows) for r in refs], [(r, rows, 2 * rows) for r in refs]


def remote_kernel(q_ref, *refs):
    *near, k_far, v_far, o_ref = refs
    rows = q_ref.shape[0]
    keys, values = halves(near)
    attend([(slice(0, rows), keys + [(k_far, 0, rows)], values + [(v_far, 0, rows)])], q_ref, o_ref)


def own_kernel(q_ref, same, other, *refs):
    *near, k_far, v_far, f_same, f_other, o_ref = refs
    rows = q_ref.shape[0]
    half = rows // 2
    jobs = []
    for i, mine in enumerate(((f_same, other), (f_other, same))):
        keys, values = halves([*mine, *near])
        here = slice(i * half, (i + 1) * half)
        jobs.append((here, keys + [(k_far, 0, rows)], values + [(v_far, 0, rows)]))
    attend(jobs, q_ref, o_ref)


def attention(kernel, query, blocks):
    rows, width = query.shape
    heads = width // HEAD_DIM
    return pl.pallas_call(
        kernel,
        out_shape=jax.ShapeDtypeStruct((rows, width + HEAD_DIM), BF),
        compiler_params=params(),
        cost_estimate=cost(16 * rows * rows * width, 4 * 2**20, 4 * rows * rows * heads),
    )(query, *blocks)


def combine_kernel(start, a_ref, b_ref, c_ref, d_ref, out):
    refs = (a_ref, b_ref, c_ref, d_ref)
    heads = a_ref.shape[1] // HEAD_DIM - 1
    here = slice(start, start + out.shape[0])
    levels = []
    for r in refs:
        s = r[here, heads * HEAD_DIM :].astype(F32)
        levels.append(s + pltpu.roll(s, HEAD_DIM - 8, 1) + pltpu.roll(s, HEAD_DIM - 16, 1))
    top = functools.reduce(jnp.maximum, levels)
    shares = [jnp.exp2(x - top) for x in levels]
    total = 1.0 / (shares[0] + shares[1] + shares[2] + shares[3])
    shares = [x * total for x in shares]
    for h in range(heads):
        cols = slice(h * HEAD_DIM, (h + 1) * HEAD_DIM)
        acc = None
        for r, w in zip(refs, shares):
            part = r[here, cols].astype(F32) * w[:, h : h + 1]
            acc = part if acc is None else acc + part
        out[:, cols] = acc.astype(BF)


def combine(parts, start):
    rows, width = parts[0].shape
    return pl.pallas_call(
        functools.partial(combine_kernel, start),
        out_shape=jax.ShapeDtypeStruct((rows // 2, width - HEAD_DIM), BF),
        compiler_params=params(),
        cost_estimate=cost(rows * width * 10, 2 * 2**20),
    )(*parts)


def project_kernel(core_ref, a_ref, b_ref, w_ref, g_ref, first_ref, second_ref, x_ref):
    half = first_ref.shape[0]
    depth = a_ref.shape[1]

    @pl.when(pl.program_id(0) == 0)
    def _():
        a, b = a_ref[...], b_ref[...]
        x_ref[:, :depth] = jnp.where(core_ref[0] == 0, a, b)
        x_ref[:, depth:] = jnp.where(core_ref[0] == 0, b, a)

    r = jnp.dot(x_ref[...], w_ref[...], preferred_element_type=F32)
    r = (r * g_ref[...]).astype(BF)
    first_ref[...] = r[:half]
    second_ref[...] = r[half:]


def project(core, mine, theirs, weight, gate, first, width):
    rows, depth = mine.shape
    tile = 512
    start = first // tile
    out = jax.ShapeDtypeStruct((rows // 2, width), BF)
    return pl.pallas_call(
        project_kernel,
        grid_spec=pltpu.PrefetchScalarGridSpec(
            num_scalar_prefetch=1,
            grid=(width // tile,),
            in_specs=[
                pl.BlockSpec((rows, depth), lambda j, c: (0, 0)),
                pl.BlockSpec((rows, depth), lambda j, c: (0, 0)),
                pl.BlockSpec((2 * depth, tile), lambda j, c: (0, start + j)),
                pl.BlockSpec((1, tile), lambda j, c: (0, start + j)),
            ],
            out_specs=[pl.BlockSpec((rows // 2, tile), lambda j, c: (0, j))] * 2,
            scratch_shapes=[pltpu.VMEM((rows, 2 * depth), BF)],
        ),
        out_shape=[out, out],
        compiler_params=params(),
        cost_estimate=cost(4 * rows * depth * width, depth * width * 4),
    )(core, mine, theirs, weight, gate)


def per_device(queries, fresh_keys, fresh_values, stale_keys, stale_values, out_weight, out_gate):
    half = queries.shape[1]
    patch = 2 * half
    head = lax.axis_index("head").astype(jnp.int32)
    core = (lax.axis_index("patch") % 2).astype(jnp.int32)
    core_table = jnp.reshape(core, (1,))
    head_table = jnp.reshape(head, (1,))

    table = jnp.stack([head, core])
    same, q_same, other = split_by_core(table, stale_keys, stale_values, queries)
    up_same, down_same = keys_along(same, 1), keys_along(same, -1)
    other = other_core(other)
    other, q_core = other[: 2 * patch], other[2 * patch :]
    up_other, down_other = keys_along(other, 1), keys_along(other, -1)

    q_got = other_half(jnp.concatenate([q_same[half:], q_core[half:]], axis=0), 0, 1)
    q_own = jnp.concatenate([q_same[:half], q_got[:half], q_core[:half], q_got[half:]], axis=0)
    q_up, q_down = queries_along(q_own, 1), queries_along(q_own, -1)
    q_far = queries_along(q_own, 2)

    k_far = keys_along(jnp.concatenate([up_same[:patch], up_other[:patch]], axis=0), 1)
    v_far = keys_along(jnp.concatenate([down_same[patch:], down_other[patch:]], axis=0), -1)

    fresh_keys, fresh_values, up_other, down_other, q_up, q_down = lax.optimization_barrier(
        (fresh_keys, fresh_values, up_other, down_other, q_up, q_down)
    )
    got = other_half(outgoing_fresh(head_table, fresh_keys[0], fresh_values[0]), 0, 1)
    blocks = [same, other, up_same, up_other, down_same, down_other, k_far, v_far]
    o_far = attention(remote_kernel, q_far, blocks)
    o_up = attention(remote_kernel, q_up, blocks)
    o_down = attention(remote_kernel, q_down, blocks)
    got, _ = lax.optimization_barrier((got, o_down))
    new_keys, new_values, f_same, f_other = assemble_fresh(
        table, fresh_keys[0], fresh_values[0], got
    )
    f_other = other_core(f_other)
    o_own = attention(own_kernel, q_own, blocks + [f_same, f_other])
    parts = (o_own, queries_along(o_far, 2), queries_along(o_up, -1), queries_along(o_down, 1))
    theirs = other_core(combine(parts, patch))
    mine = combine(parts, 0)
    pieces = []
    for start, width in ((0, 1536), (1536, out_weight.shape[2] - 1536)):
        first, second = project(core_table, mine, theirs, out_weight[0], out_gate, start, width)
        pieces.append((onward_to(first, 0), onward_to(second, 1)))
    branch = jnp.concatenate(
        [(first.astype(F32) + second.astype(F32)).astype(BF) for first, second in pieces], axis=1
    )
    return (new_keys[None], new_values[None], branch[None])


def solution(mesh):
    in_specs = (
        P("pipe", ("patch", "head"), None),
        P("pipe", ("patch", "head"), None),
        P("pipe", ("patch", "head"), None),
        P("pipe", "patch", "head"),
        P("pipe", "patch", "head"),
        P("pipe", "head", None),
        P("pipe", None),
    )
    out_specs = (
        P("pipe", "patch", "head"),
        P("pipe", "patch", "head"),
        P("pipe", ("patch", "head"), None),
    )
    return jax.shard_map(
        per_device, mesh=mesh, in_specs=in_specs, out_specs=out_specs, check_vma=False
    )
```

```python
import functools
import math
import jax
import jax.numpy as jnp
from jax import lax
from jax.experimental import pallas as pl
from jax.experimental.pallas import tpu as pltpu
from jax.sharding import PartitionSpec as P

HEAD_DIM = 128
CHIPS = 4
SCALE_LOG2 = HEAD_DIM ** (-0.5) / math.log(2.0)
BF = jnp.bfloat16
F32 = jnp.float32
VMEM_LIMIT = 20 * 1024 * 1024


def place(z, y, core):
    return ((z % CHIPS) * CHIPS + y % CHIPS) * 2 + core


def along(value, steps, core_on_y):
    pairs = []
    for z in range(CHIPS):
        for y in range(CHIPS):
            for core in range(2):
                to = place(z, y - steps, core) if core == core_on_y else place(z - steps, y, core)
                pairs.append((place(z, y, core), to))
    return lax.ppermute(value, "patch", pairs)


def keys_along(value, steps):
    return along(value, steps, 0)


def queries_along(value, steps):
    return along(value, steps, 1)


def other_core(value):
    return lax.ppermute(value, "patch", [(i, i ^ 1) for i in range(2 * CHIPS * CHIPS)])


def other_half(value, core, head):
    pairs = [
        (b * 2 + h, (b ^ core) * 2 + (h ^ head)) for b in range(2 * CHIPS * CHIPS) for h in range(2)
    ]
    return lax.ppermute(value, ("patch", "head"), pairs)


def onward_to(value, head):
    pairs = [(p * 2 + h, (1 - p) * 2 + (h ^ head)) for p in range(2) for h in range(2)]
    return lax.ppermute(value, ("pipe", "head"), pairs)


def params(limit=VMEM_LIMIT):
    return pltpu.CompilerParams(vmem_limit_bytes=limit)


def cost(flops, nbytes, trans=0):
    return pl.CostEstimate(flops=flops, bytes_accessed=nbytes, transcendentals=trans)


def split_by_core(table, keys, values, queries):
    rows, width = keys.shape[1], keys.shape[2] // 2
    few = queries.shape[1]

    def body(table_ref, k_ref, v_ref, q_ref, same_ref, q_same_ref, other_ref, sems):
        head, core = table_ref[0], table_ref[1]

        def columns(ref, i):
            return ref.at[0, :, pl.ds(pl.multiple_of(i * width, HEAD_DIM), width)]

        moves = [
            (columns(k_ref, 1 - core), other_ref.at[pl.ds(0, rows)]),
            (columns(v_ref, 1 - core), other_ref.at[pl.ds(rows, rows)]),
            (columns(q_ref, 2 * head + 1 - core), other_ref.at[pl.ds(2 * rows, few)]),
            (columns(q_ref, 2 * (1 - head) + 1 - core), other_ref.at[pl.ds(2 * rows + few, few)]),
            (columns(k_ref, core), same_ref.at[pl.ds(0, rows)]),
            (columns(v_ref, core), same_ref.at[pl.ds(rows, rows)]),
            (columns(q_ref, 2 * head + core), q_same_ref.at[pl.ds(0, few)]),
            (columns(q_ref, 2 * (1 - head) + core), q_same_ref.at[pl.ds(few, few)]),
        ]
        copies = [pltpu.make_async_copy(a, b, sems.at[i]) for i, (a, b) in enumerate(moves)]
        for c in copies:
            c.start()
        for c in copies:
            c.wait()

    vmem = pl.BlockSpec(memory_space=pltpu.VMEM)
    hbm = pl.BlockSpec(memory_space=pltpu.HBM)
    return pl.pallas_call(
        body,
        in_specs=[pl.BlockSpec(memory_space=pltpu.SMEM), hbm, hbm, hbm],
        out_specs=[vmem] * 3,
        out_shape=[
            jax.ShapeDtypeStruct((2 * rows, width), BF),
            jax.ShapeDtypeStruct((2 * few, width), BF),
            jax.ShapeDtypeStruct((2 * rows + 2 * few, width), BF),
        ],
        scratch_shapes=[pltpu.SemaphoreType.DMA((8,))],
        compiler_params=params(),
    )(table, keys, values, queries)


def outgoing_fresh(head, keys, values):
    rows, width = keys.shape[0], keys.shape[1] // 2

    def body(head_ref, k_ref, v_ref, out_ref):
        out_ref[:rows] = k_ref[...]
        out_ref[rows:] = v_ref[...]

    block = pl.BlockSpec((rows, width), lambda g, h: (0, 1 - h[0]))
    return pl.pallas_call(
        body,
        grid_spec=pltpu.PrefetchScalarGridSpec(
            num_scalar_prefetch=1,
            grid=(1,),
            in_specs=[block, block],
            out_specs=pl.BlockSpec((2 * rows, width), lambda g, h: (0, 0)),
        ),
        out_shape=jax.ShapeDtypeStruct((2 * rows, width), BF),
        compiler_params=params(),
    )(head, keys, values)


def assemble_fresh(table, keys, values, got):
    rows, width = keys.shape[0], keys.shape[1] // 2
    narrow = width // 2

    def body(table_ref, k_ref, v_ref, got_ref, nk_ref, nv_ref, same_ref, other_ref):
        head, core = table_ref[0], table_ref[1]
        for mine, at, new in ((k_ref, 0, nk_ref), (v_ref, rows, nv_ref)):
            theirs = got_ref[at : at + rows]
            low = jnp.where(head == 0, mine[...], theirs)
            high = jnp.where(head == 0, theirs, mine[...])
            new[:rows] = low
            new[rows:] = high
            for lo, x in ((2 * at, low), (2 * at + rows, high)):
                left, right = x[:, :narrow], x[:, narrow:]
                same_ref[lo : lo + rows] = jnp.where(core == 0, left, right)
                other_ref[lo : lo + rows] = jnp.where(core == 0, right, left)

    block = pl.BlockSpec((rows, width), lambda g, t: (0, t[0]))
    whole = lambda r, w: pl.BlockSpec((r, w), lambda g, t: (0, 0))
    return pl.pallas_call(
        body,
        grid_spec=pltpu.PrefetchScalarGridSpec(
            num_scalar_prefetch=1,
            grid=(1,),
            in_specs=[block, block, whole(2 * rows, width)],
            out_specs=[whole(2 * rows, width)] * 2 + [whole(4 * rows, narrow)] * 2,
        ),
        out_shape=[jax.ShapeDtypeStruct((2 * rows, width), BF)] * 2
        + [jax.ShapeDtypeStruct((4 * rows, narrow), BF)] * 2,
        compiler_params=params(),
    )(table, keys, values, got)


def nt(a, b):
    return lax.dot_general(a, b, (((1,), (1,)), ((), ())), preferred_element_type=F32)


def with_ones(v):
    return jnp.concatenate([v, jnp.ones(v.shape, BF)], axis=1)


def lanes(shape):
    return lax.broadcasted_iota(jnp.int32, shape, 1)


def attend(jobs, q_ref, o_ref):
    heads = q_ref.shape[1] // HEAD_DIM
    work = [(i, h) for h in range(heads) for i in range(len(jobs))]

    def columns(refs, h):
        cols = slice(h * HEAD_DIM, (h + 1) * HEAD_DIM)
        return jnp.concatenate([r[lo:hi, cols] for r, lo, hi in refs], axis=0)

    def product(i, h):
        here, keys, _ = jobs[i]
        return nt(q_ref[here, h * HEAD_DIM : (h + 1) * HEAD_DIM], columns(keys, h))

    shapes = [(here.stop - here.start, HEAD_DIM) for here, _, _ in jobs]
    tops = [jnp.zeros(s, F32) for s in shapes]
    totals = [jnp.ones(s, F32) for s in shapes]
    scores = product(*work[0])
    for n, (i, h) in enumerate(work):
        later = product(*work[n + 1]) if n + 1 < len(work) else None
        here, _, values = jobs[i]
        top = jnp.max(scores, axis=1, keepdims=True)
        w = jnp.exp2((scores - top) * SCALE_LOG2).astype(BF)
        part = jnp.dot(w, with_ones(columns(values, h)), preferred_element_type=F32)
        total = part[:, HEAD_DIM:]
        o_ref[here, h * HEAD_DIM : (h + 1) * HEAD_DIM] = (part[:, :HEAD_DIM] / total).astype(BF)
        at = lanes(shapes[i]) == h
        tops[i] = jnp.where(at, top, tops[i])
        totals[i] = jnp.where(at, total, totals[i])
        scores = later
    for (here, _, _), top, total in zip(jobs, tops, totals):
        level = top * SCALE_LOG2 + jnp.log2(total)
        high = level.astype(BF).astype(F32)
        rest = level - high
        middle = rest.astype(BF).astype(F32)
        packed = high + pltpu.roll(middle, 8, 1) + pltpu.roll(rest - middle, 16, 1)
        o_ref[here, heads * HEAD_DIM :] = packed.astype(BF)


def halves(refs):
    rows = refs[0].shape[0] // 2
    return [(r, 0, rows) for r in refs], [(r, rows, 2 * rows) for r in refs]


def remote_kernel(q_ref, *refs):
    *near, k_far, v_far, o_ref = refs
    rows = q_ref.shape[0]
    keys, values = halves(near)
    attend([(slice(0, rows), keys + [(k_far, 0, rows)], values + [(v_far, 0, rows)])], q_ref, o_ref)


def own_kernel(q_ref, same, other, *refs):
    *near, k_far, v_far, f_same, f_other, o_ref = refs
    rows = q_ref.shape[0]
    half = rows // 2
    jobs = []
    for i, mine in enumerate(((f_same, other), (f_other, same))):
        keys, values = halves([*mine, *near])
        here = slice(i * half, (i + 1) * half)
        jobs.append((here, keys + [(k_far, 0, rows)], values + [(v_far, 0, rows)]))
    attend(jobs, q_ref, o_ref)


def attention(kernel, query, blocks):
    rows, width = query.shape
    heads = width // HEAD_DIM
    return pl.pallas_call(
        kernel,
        out_shape=jax.ShapeDtypeStruct((rows, width + HEAD_DIM), BF),
        compiler_params=params(),
        cost_estimate=cost(16 * rows * rows * width, 4 * 2**20, 4 * rows * rows * heads),
    )(query, *blocks)


def combine_kernel(start, a_ref, b_ref, c_ref, d_ref, out):
    refs = (a_ref, b_ref, c_ref, d_ref)
    heads = a_ref.shape[1] // HEAD_DIM - 1
    here = slice(start, start + out.shape[0])
    levels = []
    for r in refs:
        s = r[here, heads * HEAD_DIM :].astype(F32)
        levels.append(s + pltpu.roll(s, HEAD_DIM - 8, 1) + pltpu.roll(s, HEAD_DIM - 16, 1))
    top = functools.reduce(jnp.maximum, levels)
    shares = [jnp.exp2(x - top) for x in levels]
    total = 1.0 / (shares[0] + shares[1] + shares[2] + shares[3])
    shares = [x * total for x in shares]
    for h in range(heads):
        cols = slice(h * HEAD_DIM, (h + 1) * HEAD_DIM)
        acc = None
        for r, w in zip(refs, shares):
            part = r[here, cols].astype(F32) * w[:, h : h + 1]
            acc = part if acc is None else acc + part
        out[:, cols] = acc.astype(BF)


def combine(parts, start):
    rows, width = parts[0].shape
    return pl.pallas_call(
        functools.partial(combine_kernel, start),
        out_shape=jax.ShapeDtypeStruct((rows // 2, width - HEAD_DIM), BF),
        compiler_params=params(),
        cost_estimate=cost(rows * width * 10, 2 * 2**20),
    )(*parts)


def project_kernel(core_ref, a_ref, b_ref, w_ref, g_ref, first_ref, second_ref, x_ref):
    half = first_ref.shape[0]
    depth = a_ref.shape[1]

    @pl.when(pl.program_id(0) == 0)
    def _():
        a, b = a_ref[...], b_ref[...]
        x_ref[:, :depth] = jnp.where(core_ref[0] == 0, a, b)
        x_ref[:, depth:] = jnp.where(core_ref[0] == 0, b, a)

    r = jnp.dot(x_ref[...], w_ref[...], preferred_element_type=F32)
    r = (r * g_ref[...]).astype(BF)
    first_ref[...] = r[:half]
    second_ref[...] = r[half:]


def project(core, mine, theirs, weight, gate, first, width):
    rows, depth = mine.shape
    tile = 512
    start = first // tile
    out = jax.ShapeDtypeStruct((rows // 2, width), BF)
    return pl.pallas_call(
        project_kernel,
        grid_spec=pltpu.PrefetchScalarGridSpec(
            num_scalar_prefetch=1,
            grid=(width // tile,),
            in_specs=[
                pl.BlockSpec((rows, depth), lambda j, c: (0, 0)),
                pl.BlockSpec((rows, depth), lambda j, c: (0, 0)),
                pl.BlockSpec((2 * depth, tile), lambda j, c: (0, start + j)),
                pl.BlockSpec((1, tile), lambda j, c: (0, start + j)),
            ],
            out_specs=[pl.BlockSpec((rows // 2, tile), lambda j, c: (0, j))] * 2,
            scratch_shapes=[pltpu.VMEM((rows, 2 * depth), BF)],
        ),
        out_shape=[out, out],
        compiler_params=params(),
        cost_estimate=cost(4 * rows * depth * width, depth * width * 4),
    )(core, mine, theirs, weight, gate)


def per_device(queries, fresh_keys, fresh_values, stale_keys, stale_values, out_weight, out_gate):
    half = queries.shape[1]
    patch = 2 * half
    head = lax.axis_index("head").astype(jnp.int32)
    core = (lax.axis_index("patch") % 2).astype(jnp.int32)
    core_table = jnp.reshape(core, (1,))
    head_table = jnp.reshape(head, (1,))

    table = jnp.stack([head, core])
    same, q_same, other = split_by_core(table, stale_keys, stale_values, queries)
    up_same, down_same = keys_along(same, 1), keys_along(same, -1)
    other = other_core(other)
    other, q_core = other[: 2 * patch], other[2 * patch :]
    up_other, down_other = keys_along(other, 1), keys_along(other, -1)

    q_got = other_half(jnp.concatenate([q_same[half:], q_core[half:]], axis=0), 0, 1)
    q_own = jnp.concatenate([q_same[:half], q_got[:half], q_core[:half], q_got[half:]], axis=0)
    q_up, q_down = queries_along(q_own, 1), queries_along(q_own, -1)
    q_far = queries_along(q_own, 2)

    k_far = keys_along(jnp.concatenate([up_same[:patch], up_other[:patch]], axis=0), 1)
    v_far = keys_along(jnp.concatenate([down_same[patch:], down_other[patch:]], axis=0), -1)

    fresh_keys, fresh_values, up_other, down_other, q_far = lax.optimization_barrier(
        (fresh_keys, fresh_values, up_other, down_other, q_far)
    )
    got = other_half(outgoing_fresh(head_table, fresh_keys[0], fresh_values[0]), 0, 1)
    blocks = [same, other, up_same, up_other, down_same, down_other, k_far, v_far]
    o_far = attention(remote_kernel, q_far, blocks)
    o_up = attention(remote_kernel, q_up, blocks)
    o_down = attention(remote_kernel, q_down, blocks)
    far, up, down = queries_along(o_far, 2), queries_along(o_up, -1), queries_along(o_down, 1)
    got, _, _, _ = lax.optimization_barrier((got, o_far, o_up, o_down))
    new_keys, new_values, f_same, f_other = assemble_fresh(
        table, fresh_keys[0], fresh_values[0], got
    )
    f_other = other_core(f_other)
    q_own, far, down = lax.optimization_barrier((q_own, far, down))
    o_own = attention(own_kernel, q_own, blocks + [f_same, f_other])
    parts = (o_own, far, up, down)
    theirs = other_core(combine(parts, patch))
    mine = combine(parts, 0)
    pieces = []
    for start, width in ((0, 1536), (1536, out_weight.shape[2] - 1536)):
        first, second = project(core_table, mine, theirs, out_weight[0], out_gate, start, width)
        pieces.append((onward_to(first, 0), onward_to(second, 1)))
    branch = jnp.concatenate(
        [(first.astype(F32) + second.astype(F32)).astype(BF) for first, second in pieces], axis=1
    )
    return (new_keys[None], new_values[None], branch[None])


def solution(mesh):
    in_specs = (
        P("pipe", ("patch", "head"), None),
        P("pipe", ("patch", "head"), None),
        P("pipe", ("patch", "head"), None),
        P("pipe", "patch", "head"),
        P("pipe", "patch", "head"),
        P("pipe", "head", None),
        P("pipe", None),
    )
    out_specs = (
        P("pipe", "patch", "head"),
        P("pipe", "patch", "head"),
        P("pipe", ("patch", "head"), None),
    )
    return jax.shard_map(
        per_device, mesh=mesh, in_specs=in_specs, out_specs=out_specs, check_vma=False
    )
```

```python
import functools
import math
import jax
import jax.numpy as jnp
from jax import lax
from jax.experimental import pallas as pl
from jax.experimental.pallas import tpu as pltpu
from jax.sharding import PartitionSpec as P

HEAD_DIM = 128
CHIPS = 4
SCALE_LOG2 = HEAD_DIM ** (-0.5) / math.log(2.0)
BF = jnp.bfloat16
F32 = jnp.float32
VMEM_LIMIT = 20 * 1024 * 1024


def place(z, y, core):
    return ((z % CHIPS) * CHIPS + y % CHIPS) * 2 + core


def along(value, steps, core_on_y):
    pairs = []
    for z in range(CHIPS):
        for y in range(CHIPS):
            for core in range(2):
                to = place(z, y + steps, core) if core == core_on_y else place(z + steps, y, core)
                pairs.append((place(z, y, core), to))
    return lax.ppermute(value, "patch", pairs)


def keys_along(value, steps):
    return along(value, steps, 0)


def queries_along(value, steps):
    return along(value, steps, 1)


def other_core(value):
    return lax.ppermute(value, "patch", [(i, i ^ 1) for i in range(2 * CHIPS * CHIPS)])


def other_half(value, core, head):
    pairs = [
        (b * 2 + h, (b ^ core) * 2 + (h ^ head)) for b in range(2 * CHIPS * CHIPS) for h in range(2)
    ]
    return lax.ppermute(value, ("patch", "head"), pairs)


def onward_to(value, head):
    pairs = [(p * 2 + h, (1 - p) * 2 + (h ^ head)) for p in range(2) for h in range(2)]
    return lax.ppermute(value, ("pipe", "head"), pairs)


def params(limit=VMEM_LIMIT):
    return pltpu.CompilerParams(vmem_limit_bytes=limit)


def cost(flops, nbytes, trans=0):
    return pl.CostEstimate(flops=flops, bytes_accessed=nbytes, transcendentals=trans)


def split_by_core(table, keys, values, queries):
    rows, width = keys.shape[1], keys.shape[2] // 2
    few = queries.shape[1]

    def body(table_ref, k_ref, v_ref, q_ref, same_ref, q_same_ref, other_ref, sems):
        head, core = table_ref[0], table_ref[1]

        def columns(ref, i):
            return ref.at[0, :, pl.ds(pl.multiple_of(i * width, HEAD_DIM), width)]

        moves = [
            (columns(k_ref, 1 - core), other_ref.at[pl.ds(0, rows)]),
            (columns(v_ref, 1 - core), other_ref.at[pl.ds(rows, rows)]),
            (columns(q_ref, 2 * head + 1 - core), other_ref.at[pl.ds(2 * rows, few)]),
            (columns(q_ref, 2 * (1 - head) + 1 - core), other_ref.at[pl.ds(2 * rows + few, few)]),
            (columns(k_ref, core), same_ref.at[pl.ds(0, rows)]),
            (columns(v_ref, core), same_ref.at[pl.ds(rows, rows)]),
            (columns(q_ref, 2 * head + core), q_same_ref.at[pl.ds(0, few)]),
            (columns(q_ref, 2 * (1 - head) + core), q_same_ref.at[pl.ds(few, few)]),
        ]
        copies = [pltpu.make_async_copy(a, b, sems.at[i]) for i, (a, b) in enumerate(moves)]
        for c in copies:
            c.start()
        for c in copies:
            c.wait()

    vmem = pl.BlockSpec(memory_space=pltpu.VMEM)
    hbm = pl.BlockSpec(memory_space=pltpu.HBM)
    return pl.pallas_call(
        body,
        in_specs=[pl.BlockSpec(memory_space=pltpu.SMEM), hbm, hbm, hbm],
        out_specs=[vmem] * 3,
        out_shape=[
            jax.ShapeDtypeStruct((2 * rows, width), BF),
            jax.ShapeDtypeStruct((2 * few, width), BF),
            jax.ShapeDtypeStruct((2 * rows + 2 * few, width), BF),
        ],
        scratch_shapes=[pltpu.SemaphoreType.DMA((8,))],
        compiler_params=params(),
    )(table, keys, values, queries)


def outgoing_fresh(head, keys, values):
    rows, width = keys.shape[0], keys.shape[1] // 2

    def body(head_ref, k_ref, v_ref, out_ref):
        out_ref[:rows] = k_ref[...]
        out_ref[rows:] = v_ref[...]

    block = pl.BlockSpec((rows, width), lambda g, h: (0, 1 - h[0]))
    return pl.pallas_call(
        body,
        grid_spec=pltpu.PrefetchScalarGridSpec(
            num_scalar_prefetch=1,
            grid=(1,),
            in_specs=[block, block],
            out_specs=pl.BlockSpec((2 * rows, width), lambda g, h: (0, 0)),
        ),
        out_shape=jax.ShapeDtypeStruct((2 * rows, width), BF),
        compiler_params=params(),
    )(head, keys, values)


def fresh_by_core(table, keys, values, got):
    rows, width = keys.shape[0], keys.shape[1] // 2
    narrow = width // 2

    def body(table_ref, k_ref, v_ref, got_ref, same_ref, other_ref):
        head, core = table_ref[0], table_ref[1]
        for mine, at in ((k_ref, 0), (v_ref, rows)):
            theirs = got_ref[at : at + rows]
            low = jnp.where(head == 0, mine[...], theirs)
            high = jnp.where(head == 0, theirs, mine[...])
            for lo, x in ((2 * at, low), (2 * at + rows, high)):
                left, right = x[:, :narrow], x[:, narrow:]
                same_ref[lo : lo + rows] = jnp.where(core == 0, left, right)
                other_ref[lo : lo + rows] = jnp.where(core == 0, right, left)

    block = pl.BlockSpec((rows, width), lambda g, t: (0, t[0]))
    whole = lambda r, w: pl.BlockSpec((r, w), lambda g, t: (0, 0))
    return pl.pallas_call(
        body,
        grid_spec=pltpu.PrefetchScalarGridSpec(
            num_scalar_prefetch=1,
            grid=(1,),
            in_specs=[block, block, whole(2 * rows, width)],
            out_specs=[whole(4 * rows, narrow)] * 2,
        ),
        out_shape=[jax.ShapeDtypeStruct((4 * rows, narrow), BF)] * 2,
        compiler_params=params(),
    )(table, keys, values, got)


def new_in_order(table, keys, values, got):
    rows, width = keys.shape[0], keys.shape[1] // 2

    def body(table_ref, k_ref, v_ref, got_ref, nk_ref, nv_ref):
        head = table_ref[0]
        for mine, at, new in ((k_ref, 0, nk_ref), (v_ref, rows, nv_ref)):
            theirs = got_ref[at : at + rows]
            new[:rows] = jnp.where(head == 0, mine[...], theirs)
            new[rows:] = jnp.where(head == 0, theirs, mine[...])

    block = pl.BlockSpec((rows, width), lambda g, t: (0, t[0]))
    whole = lambda r, w: pl.BlockSpec((r, w), lambda g, t: (0, 0))
    return pl.pallas_call(
        body,
        grid_spec=pltpu.PrefetchScalarGridSpec(
            num_scalar_prefetch=1,
            grid=(1,),
            in_specs=[block, block, whole(2 * rows, width)],
            out_specs=[whole(2 * rows, width)] * 2,
        ),
        out_shape=[jax.ShapeDtypeStruct((2 * rows, width), BF)] * 2,
        compiler_params=params(),
    )(table, keys, values, got)


def nt(a, b):
    return lax.dot_general(a, b, (((1,), (1,)), ((), ())), preferred_element_type=F32)


def with_ones(v):
    return jnp.concatenate([v, jnp.ones(v.shape, BF)], axis=1)


def lanes(shape):
    return lax.broadcasted_iota(jnp.int32, shape, 1)


def attend(jobs, q_ref, o_ref):
    heads = q_ref.shape[1] // HEAD_DIM
    work = [(i, h) for h in range(heads) for i in range(len(jobs))]

    def columns(refs, h):
        cols = slice(h * HEAD_DIM, (h + 1) * HEAD_DIM)
        return jnp.concatenate([r[lo:hi, cols] for r, lo, hi in refs], axis=0)

    def product(i, h):
        here, keys, _ = jobs[i]
        return nt(q_ref[here, h * HEAD_DIM : (h + 1) * HEAD_DIM], columns(keys, h))

    shapes = [(here.stop - here.start, HEAD_DIM) for here, _, _ in jobs]
    tops = [jnp.zeros(s, F32) for s in shapes]
    totals = [jnp.ones(s, F32) for s in shapes]
    scores = product(*work[0])
    for n, (i, h) in enumerate(work):
        later = product(*work[n + 1]) if n + 1 < len(work) else None
        here, _, values = jobs[i]
        top = jnp.max(scores, axis=1, keepdims=True)
        w = jnp.exp2((scores - top) * SCALE_LOG2).astype(BF)
        part = jnp.dot(w, with_ones(columns(values, h)), preferred_element_type=F32)
        total = part[:, HEAD_DIM:]
        o_ref[here, h * HEAD_DIM : (h + 1) * HEAD_DIM] = (part[:, :HEAD_DIM] / total).astype(BF)
        at = lanes(shapes[i]) == h
        tops[i] = jnp.where(at, top, tops[i])
        totals[i] = jnp.where(at, total, totals[i])
        scores = later
    for (here, _, _), top, total in zip(jobs, tops, totals):
        level = top * SCALE_LOG2 + jnp.log2(total)
        high = level.astype(BF).astype(F32)
        rest = level - high
        middle = rest.astype(BF).astype(F32)
        packed = high + pltpu.roll(middle, 8, 1) + pltpu.roll(rest - middle, 16, 1)
        o_ref[here, heads * HEAD_DIM :] = packed.astype(BF)


def halves(refs):
    rows = refs[0].shape[0] // 2
    return [(r, 0, rows) for r in refs], [(r, rows, 2 * rows) for r in refs]


def remote_kernel(q_ref, *refs):
    *near, k_far, v_far, o_ref = refs
    rows = q_ref.shape[0]
    keys, values = halves(near)
    attend([(slice(0, rows), keys + [(k_far, 0, rows)], values + [(v_far, 0, rows)])], q_ref, o_ref)


def own_kernel(q_ref, same, other, *refs):
    *near, k_far, v_far, f_same, f_other, o_ref = refs
    rows = q_ref.shape[0]
    half = rows // 2
    jobs = []
    for i, mine in enumerate(((f_same, other), (f_other, same))):
        keys, values = halves([*mine, *near])
        here = slice(i * half, (i + 1) * half)
        jobs.append((here, keys + [(k_far, 0, rows)], values + [(v_far, 0, rows)]))
    attend(jobs, q_ref, o_ref)


def attention(kernel, query, blocks):
    rows, width = query.shape
    heads = width // HEAD_DIM
    return pl.pallas_call(
        kernel,
        out_shape=jax.ShapeDtypeStruct((rows, width + HEAD_DIM), BF),
        compiler_params=params(),
        cost_estimate=cost(16 * rows * rows * width, 4 * 2**20, 4 * rows * rows * heads),
    )(query, *blocks)


def combine_kernel(start, a_ref, b_ref, c_ref, d_ref, out):
    refs = (a_ref, b_ref, c_ref, d_ref)
    heads = a_ref.shape[1] // HEAD_DIM - 1
    here = slice(start, start + out.shape[0])
    levels = []
    for r in refs:
        s = r[here, heads * HEAD_DIM :].astype(F32)
        levels.append(s + pltpu.roll(s, HEAD_DIM - 8, 1) + pltpu.roll(s, HEAD_DIM - 16, 1))
    top = functools.reduce(jnp.maximum, levels)
    shares = [jnp.exp2(x - top) for x in levels]
    total = 1.0 / (shares[0] + shares[1] + shares[2] + shares[3])
    shares = [x * total for x in shares]
    for h in range(heads):
        cols = slice(h * HEAD_DIM, (h + 1) * HEAD_DIM)
        acc = None
        for r, w in zip(refs, shares):
            part = r[here, cols].astype(F32) * w[:, h : h + 1]
            acc = part if acc is None else acc + part
        out[:, cols] = acc.astype(BF)


def combine(parts, start):
    rows, width = parts[0].shape
    return pl.pallas_call(
        functools.partial(combine_kernel, start),
        out_shape=jax.ShapeDtypeStruct((rows // 2, width - HEAD_DIM), BF),
        compiler_params=params(),
        cost_estimate=cost(rows * width * 10, 2 * 2**20),
    )(*parts)


def project_kernel(core_ref, a_ref, b_ref, w_ref, g_ref, first_ref, second_ref, x_ref):
    half = first_ref.shape[0]
    depth = a_ref.shape[1]

    @pl.when(pl.program_id(0) == 0)
    def _():
        a, b = a_ref[...], b_ref[...]
        x_ref[:, :depth] = jnp.where(core_ref[0] == 0, a, b)
        x_ref[:, depth:] = jnp.where(core_ref[0] == 0, b, a)

    r = jnp.dot(x_ref[...], w_ref[...], preferred_element_type=F32)
    r = (r * g_ref[...]).astype(BF)
    first_ref[...] = r[:half]
    second_ref[...] = r[half:]


def project(core, mine, theirs, weight, gate, first, width):
    rows, depth = mine.shape
    tile = 512
    start = first // tile
    out = jax.ShapeDtypeStruct((rows // 2, width), BF)
    return pl.pallas_call(
        project_kernel,
        grid_spec=pltpu.PrefetchScalarGridSpec(
            num_scalar_prefetch=1,
            grid=(width // tile,),
            in_specs=[
                pl.BlockSpec((rows, depth), lambda j, c: (0, 0)),
                pl.BlockSpec((rows, depth), lambda j, c: (0, 0)),
                pl.BlockSpec((2 * depth, tile), lambda j, c: (0, start + j)),
                pl.BlockSpec((1, tile), lambda j, c: (0, start + j)),
            ],
            out_specs=[pl.BlockSpec((rows // 2, tile), lambda j, c: (0, j))] * 2,
            scratch_shapes=[pltpu.VMEM((rows, 2 * depth), BF)],
        ),
        out_shape=[out, out],
        compiler_params=params(),
        cost_estimate=cost(4 * rows * depth * width, depth * width * 4),
    )(core, mine, theirs, weight, gate)


def per_device(queries, fresh_keys, fresh_values, stale_keys, stale_values, out_weight, out_gate):
    half = queries.shape[1]
    patch = 2 * half
    head = lax.axis_index("head").astype(jnp.int32)
    core = (lax.axis_index("patch") % 2).astype(jnp.int32)
    core_table = jnp.reshape(core, (1,))
    head_table = jnp.reshape(head, (1,))

    table = jnp.stack([head, core])
    same, q_same, other = split_by_core(table, stale_keys, stale_values, queries)
    up_same, down_same = keys_along(same, 1), keys_along(same, -1)
    other = other_core(other)
    other, q_core = other[: 2 * patch], other[2 * patch :]
    up_other, down_other = keys_along(other, 1), keys_along(other, -1)

    q_got = other_half(jnp.concatenate([q_same[half:], q_core[half:]], axis=0), 0, 1)
    q_own = jnp.concatenate([q_same[:half], q_got[:half], q_core[:half], q_got[half:]], axis=0)
    q_up, q_down = queries_along(q_own, 1), queries_along(q_own, -1)
    q_far = queries_along(q_own, 2)

    k_far = keys_along(jnp.concatenate([up_same[:patch], up_other[:patch]], axis=0), 1)
    v_far = keys_along(jnp.concatenate([down_same[patch:], down_other[patch:]], axis=0), -1)

    fresh_keys, fresh_values, up_other, down_other, q_far = lax.optimization_barrier(
        (fresh_keys, fresh_values, up_other, down_other, q_far)
    )
    got = other_half(outgoing_fresh(head_table, fresh_keys[0], fresh_values[0]), 0, 1)
    blocks = [same, other, up_same, up_other, down_same, down_other, k_far, v_far]
    o_far = attention(remote_kernel, q_far, blocks)
    o_up = attention(remote_kernel, q_up, blocks)
    o_down = attention(remote_kernel, q_down, blocks)
    far, up, down = queries_along(o_far, 2), queries_along(o_up, -1), queries_along(o_down, 1)
    got, _, _, _ = lax.optimization_barrier((got, o_far, o_up, o_down))
    f_same, f_other = fresh_by_core(table, fresh_keys[0], fresh_values[0], got)
    f_other = other_core(f_other)
    q_own, far, down = lax.optimization_barrier((q_own, far, down))
    o_own = attention(own_kernel, q_own, blocks + [f_same, f_other])
    parts = (o_own, far, up, down)
    theirs = other_core(combine(parts, patch))
    mine = combine(parts, 0)
    pieces = []
    for start, width in ((0, 1536), (1536, out_weight.shape[2] - 1536)):
        first, second = project(core_table, mine, theirs, out_weight[0], out_gate, start, width)
        pieces.append((onward_to(first, 0), onward_to(second, 1)))
    branch = jnp.concatenate(
        [(first.astype(F32) + second.astype(F32)).astype(BF) for first, second in pieces], axis=1
    )
    new_keys, new_values = new_in_order(table, fresh_keys[0], fresh_values[0], got)
    return (new_keys[None], new_values[None], branch[None])


def solution(mesh):
    in_specs = (
        P("pipe", ("patch", "head"), None),
        P("pipe", ("patch", "head"), None),
        P("pipe", ("patch", "head"), None),
        P("pipe", "patch", "head"),
        P("pipe", "patch", "head"),
        P("pipe", "head", None),
        P("pipe", None),
    )
    out_specs = (
        P("pipe", "patch", "head"),
        P("pipe", "patch", "head"),
        P("pipe", ("patch", "head"), None),
    )
    return jax.shard_map(
        per_device, mesh=mesh, in_specs=in_specs, out_specs=out_specs, check_vma=False
    )
```

```python
import functools
import math
import jax
import jax.numpy as jnp
from jax import lax
from jax.experimental import pallas as pl
from jax.experimental.pallas import tpu as pltpu
from jax.sharding import PartitionSpec as P

HEAD_DIM = 128
CHIPS = 4
SCALE_LOG2 = HEAD_DIM ** (-0.5) / math.log(2.0)
BF = jnp.bfloat16
F32 = jnp.float32
VMEM_LIMIT = 20 * 1024 * 1024


def place(z, y, core):
    return ((z % CHIPS) * CHIPS + y % CHIPS) * 2 + core


def along(value, steps, core_on_y):
    pairs = []
    for z in range(CHIPS):
        for y in range(CHIPS):
            for core in range(2):
                to = place(z, y + steps, core) if core == core_on_y else place(z + steps, y, core)
                pairs.append((place(z, y, core), to))
    return lax.ppermute(value, "patch", pairs)


def keys_along(value, steps):
    return along(value, steps, 0)


def queries_along(value, steps):
    return along(value, steps, 1)


def other_core(value):
    return lax.ppermute(value, "patch", [(i, i ^ 1) for i in range(2 * CHIPS * CHIPS)])


def other_half(value, core, head):
    pairs = [
        (b * 2 + h, (b ^ core) * 2 + (h ^ head)) for b in range(2 * CHIPS * CHIPS) for h in range(2)
    ]
    return lax.ppermute(value, ("patch", "head"), pairs)


def onward_to(value, head):
    pairs = [(p * 2 + h, (1 - p) * 2 + (h ^ head)) for p in range(2) for h in range(2)]
    return lax.ppermute(value, ("pipe", "head"), pairs)


def params(limit=VMEM_LIMIT):
    return pltpu.CompilerParams(vmem_limit_bytes=limit)


def cost(flops, nbytes, trans=0):
    return pl.CostEstimate(flops=flops, bytes_accessed=nbytes, transcendentals=trans)


def split_by_core(table, keys, values, queries):
    rows, width = keys.shape[1], keys.shape[2] // 2
    few = queries.shape[1]

    def body(table_ref, k_ref, v_ref, q_ref, same_ref, q_same_ref, other_ref, sems):
        head, core = table_ref[0], table_ref[1]

        def columns(ref, i):
            return ref.at[0, :, pl.ds(pl.multiple_of(i * width, HEAD_DIM), width)]

        moves = [
            (columns(k_ref, 1 - core), other_ref.at[pl.ds(0, rows)]),
            (columns(v_ref, 1 - core), other_ref.at[pl.ds(rows, rows)]),
            (columns(q_ref, 2 * head + 1 - core), other_ref.at[pl.ds(2 * rows, few)]),
            (columns(q_ref, 2 * (1 - head) + 1 - core), other_ref.at[pl.ds(2 * rows + few, few)]),
            (columns(k_ref, core), same_ref.at[pl.ds(0, rows)]),
            (columns(v_ref, core), same_ref.at[pl.ds(rows, rows)]),
            (columns(q_ref, 2 * head + core), q_same_ref.at[pl.ds(0, few)]),
            (columns(q_ref, 2 * (1 - head) + core), q_same_ref.at[pl.ds(few, few)]),
        ]
        copies = [pltpu.make_async_copy(a, b, sems.at[i]) for i, (a, b) in enumerate(moves)]
        for c in copies:
            c.start()
        for c in copies:
            c.wait()

    vmem = pl.BlockSpec(memory_space=pltpu.VMEM)
    hbm = pl.BlockSpec(memory_space=pltpu.HBM)
    return pl.pallas_call(
        body,
        in_specs=[pl.BlockSpec(memory_space=pltpu.SMEM), hbm, hbm, hbm],
        out_specs=[vmem] * 3,
        out_shape=[
            jax.ShapeDtypeStruct((2 * rows, width), BF),
            jax.ShapeDtypeStruct((2 * few, width), BF),
            jax.ShapeDtypeStruct((2 * rows + 2 * few, width), BF),
        ],
        scratch_shapes=[pltpu.SemaphoreType.DMA((8,))],
        compiler_params=params(),
    )(table, keys, values, queries)


def outgoing_fresh(head, keys, values):
    rows, width = keys.shape[0], keys.shape[1] // 2

    def body(head_ref, k_ref, v_ref, out_ref):
        out_ref[:rows] = k_ref[...]
        out_ref[rows:] = v_ref[...]

    block = pl.BlockSpec((rows, width), lambda g, h: (0, 1 - h[0]))
    return pl.pallas_call(
        body,
        grid_spec=pltpu.PrefetchScalarGridSpec(
            num_scalar_prefetch=1,
            grid=(1,),
            in_specs=[block, block],
            out_specs=pl.BlockSpec((2 * rows, width), lambda g, h: (0, 0)),
        ),
        out_shape=jax.ShapeDtypeStruct((2 * rows, width), BF),
        compiler_params=params(),
    )(head, keys, values)


def fresh_by_core(table, keys, values, got):
    rows, width = keys.shape[0], keys.shape[1] // 2
    narrow = width // 2

    def body(table_ref, k_ref, v_ref, got_ref, same_ref, other_ref):
        head, core = table_ref[0], table_ref[1]
        for mine, at in ((k_ref, 0), (v_ref, rows)):
            theirs = got_ref[at : at + rows]
            low = jnp.where(head == 0, mine[...], theirs)
            high = jnp.where(head == 0, theirs, mine[...])
            for lo, x in ((2 * at, low), (2 * at + rows, high)):
                left, right = x[:, :narrow], x[:, narrow:]
                same_ref[lo : lo + rows] = jnp.where(core == 0, left, right)
                other_ref[lo : lo + rows] = jnp.where(core == 0, right, left)

    block = pl.BlockSpec((rows, width), lambda g, t: (0, t[0]))
    whole = lambda r, w: pl.BlockSpec((r, w), lambda g, t: (0, 0))
    return pl.pallas_call(
        body,
        grid_spec=pltpu.PrefetchScalarGridSpec(
            num_scalar_prefetch=1,
            grid=(1,),
            in_specs=[block, block, whole(2 * rows, width)],
            out_specs=[whole(4 * rows, narrow)] * 2,
        ),
        out_shape=[jax.ShapeDtypeStruct((4 * rows, narrow), BF)] * 2,
        compiler_params=params(),
    )(table, keys, values, got)


def new_in_order(table, keys, values, got):
    rows, width = keys.shape[0], keys.shape[1] // 2

    def body(table_ref, k_ref, v_ref, got_ref, nk_ref, nv_ref):
        head = table_ref[0]
        for mine, at, new in ((k_ref, 0, nk_ref), (v_ref, rows, nv_ref)):
            theirs = got_ref[at : at + rows]
            new[:rows] = jnp.where(head == 0, mine[...], theirs)
            new[rows:] = jnp.where(head == 0, theirs, mine[...])

    block = pl.BlockSpec((rows, width), lambda g, t: (0, t[0]))
    whole = lambda r, w: pl.BlockSpec((r, w), lambda g, t: (0, 0))
    return pl.pallas_call(
        body,
        grid_spec=pltpu.PrefetchScalarGridSpec(
            num_scalar_prefetch=1,
            grid=(1,),
            in_specs=[block, block, whole(2 * rows, width)],
            out_specs=[whole(2 * rows, width)] * 2,
        ),
        out_shape=[jax.ShapeDtypeStruct((2 * rows, width), BF)] * 2,
        compiler_params=params(),
    )(table, keys, values, got)


def nt(a, b):
    return lax.dot_general(a, b, (((1,), (1,)), ((), ())), preferred_element_type=F32)


def with_ones(v):
    return jnp.concatenate([v, jnp.ones(v.shape, BF)], axis=1)


def lanes(shape):
    return lax.broadcasted_iota(jnp.int32, shape, 1)


def attend(jobs, q_ref, o_ref):
    heads = q_ref.shape[1] // HEAD_DIM
    work = [(i, h) for h in range(heads) for i in range(len(jobs))]

    def columns(refs, h):
        cols = slice(h * HEAD_DIM, (h + 1) * HEAD_DIM)
        return jnp.concatenate([r[lo:hi, cols] for r, lo, hi in refs], axis=0)

    def product(i, h):
        here, keys, _ = jobs[i]
        return nt(q_ref[here, h * HEAD_DIM : (h + 1) * HEAD_DIM], columns(keys, h))

    shapes = [(here.stop - here.start, HEAD_DIM) for here, _, _ in jobs]
    tops = [jnp.zeros(s, F32) for s in shapes]
    totals = [jnp.ones(s, F32) for s in shapes]
    scores = product(*work[0])
    for n, (i, h) in enumerate(work):
        later = product(*work[n + 1]) if n + 1 < len(work) else None
        here, _, values = jobs[i]
        top = jnp.max(scores, axis=1, keepdims=True)
        w = jnp.exp2((scores - top) * SCALE_LOG2).astype(BF)
        part = jnp.dot(w, with_ones(columns(values, h)), preferred_element_type=F32)
        total = part[:, HEAD_DIM:]
        o_ref[here, h * HEAD_DIM : (h + 1) * HEAD_DIM] = (part[:, :HEAD_DIM] / total).astype(BF)
        at = lanes(shapes[i]) == h
        tops[i] = jnp.where(at, top, tops[i])
        totals[i] = jnp.where(at, total, totals[i])
        scores = later
    for (here, _, _), top, total in zip(jobs, tops, totals):
        level = top * SCALE_LOG2 + jnp.log2(total)
        high = level.astype(BF).astype(F32)
        rest = level - high
        middle = rest.astype(BF).astype(F32)
        packed = high + pltpu.roll(middle, 8, 1) + pltpu.roll(rest - middle, 16, 1)
        o_ref[here, heads * HEAD_DIM :] = packed.astype(BF)


def halves(refs):
    rows = refs[0].shape[0] // 2
    return [(r, 0, rows) for r in refs], [(r, rows, 2 * rows) for r in refs]


def remote_kernel(q_ref, *refs):
    *near, k_far, v_far, o_ref = refs
    rows = q_ref.shape[0]
    keys, values = halves(near)
    attend([(slice(0, rows), keys + [(k_far, 0, rows)], values + [(v_far, 0, rows)])], q_ref, o_ref)


def own_kernel(q_ref, same, other, *refs):
    *near, k_far, v_far, f_same, f_other, o_ref = refs
    rows = q_ref.shape[0]
    half = rows // 2
    jobs = []
    for i, mine in enumerate(((f_same, other), (f_other, same))):
        keys, values = halves([*mine, *near])
        here = slice(i * half, (i + 1) * half)
        jobs.append((here, keys + [(k_far, 0, rows)], values + [(v_far, 0, rows)]))
    attend(jobs, q_ref, o_ref)


def attention(kernel, query, blocks):
    rows, width = query.shape
    heads = width // HEAD_DIM
    return pl.pallas_call(
        kernel,
        out_shape=jax.ShapeDtypeStruct((rows, width + HEAD_DIM), BF),
        compiler_params=params(),
        cost_estimate=cost(16 * rows * rows * width, 4 * 2**20, 4 * rows * rows * heads),
    )(query, *blocks)


def combine_kernel(start, a_ref, b_ref, c_ref, d_ref, out):
    refs = (a_ref, b_ref, c_ref, d_ref)
    heads = a_ref.shape[1] // HEAD_DIM - 1
    here = slice(start, start + out.shape[0])
    levels = []
    for r in refs:
        s = r[here, heads * HEAD_DIM :].astype(F32)
        levels.append(s + pltpu.roll(s, HEAD_DIM - 8, 1) + pltpu.roll(s, HEAD_DIM - 16, 1))
    top = functools.reduce(jnp.maximum, levels)
    shares = [jnp.exp2(x - top) for x in levels]
    total = 1.0 / (shares[0] + shares[1] + shares[2] + shares[3])
    shares = [x * total for x in shares]
    for h in range(heads):
        cols = slice(h * HEAD_DIM, (h + 1) * HEAD_DIM)
        acc = None
        for r, w in zip(refs, shares):
            part = r[here, cols].astype(F32) * w[:, h : h + 1]
            acc = part if acc is None else acc + part
        out[:, cols] = acc.astype(BF)


def combine(parts, start):
    rows, width = parts[0].shape
    return pl.pallas_call(
        functools.partial(combine_kernel, start),
        out_shape=jax.ShapeDtypeStruct((rows // 2, width - HEAD_DIM), BF),
        compiler_params=params(),
        cost_estimate=cost(rows * width * 10, 2 * 2**20),
    )(*parts)


def project_kernel(core_ref, a_ref, b_ref, w_ref, g_ref, first_ref, second_ref, x_ref):
    half = first_ref.shape[0]
    depth = a_ref.shape[1]

    @pl.when(pl.program_id(0) == 0)
    def _():
        a, b = a_ref[...], b_ref[...]
        x_ref[:, :depth] = jnp.where(core_ref[0] == 0, a, b)
        x_ref[:, depth:] = jnp.where(core_ref[0] == 0, b, a)

    r = jnp.dot(x_ref[...], w_ref[...], preferred_element_type=F32)
    r = (r * g_ref[...]).astype(BF)
    first_ref[...] = r[:half]
    second_ref[...] = r[half:]


def project(core, mine, theirs, weight, gate, first, width):
    rows, depth = mine.shape
    tile = 512
    start = first // tile
    out = jax.ShapeDtypeStruct((rows // 2, width), BF)
    return pl.pallas_call(
        project_kernel,
        grid_spec=pltpu.PrefetchScalarGridSpec(
            num_scalar_prefetch=1,
            grid=(width // tile,),
            in_specs=[
                pl.BlockSpec((rows, depth), lambda j, c: (0, 0)),
                pl.BlockSpec((rows, depth), lambda j, c: (0, 0)),
                pl.BlockSpec((2 * depth, tile), lambda j, c: (0, start + j)),
                pl.BlockSpec((1, tile), lambda j, c: (0, start + j)),
            ],
            out_specs=[pl.BlockSpec((rows // 2, tile), lambda j, c: (0, j))] * 2,
            scratch_shapes=[pltpu.VMEM((rows, 2 * depth), BF)],
        ),
        out_shape=[out, out],
        compiler_params=params(),
        cost_estimate=cost(4 * rows * depth * width, depth * width * 4),
    )(core, mine, theirs, weight, gate)


def per_device(queries, fresh_keys, fresh_values, stale_keys, stale_values, out_weight, out_gate):
    half = queries.shape[1]
    patch = 2 * half
    head = lax.axis_index("head").astype(jnp.int32)
    core = (lax.axis_index("patch") % 2).astype(jnp.int32)
    core_table = jnp.reshape(core, (1,))
    head_table = jnp.reshape(head, (1,))

    table = jnp.stack([head, core])
    same, q_same, other = split_by_core(table, stale_keys, stale_values, queries)
    up_same, down_same = keys_along(same, 1), keys_along(same, -1)
    other = other_core(other)
    other, q_core = other[: 2 * patch], other[2 * patch :]
    up_other, down_other = keys_along(other, 1), keys_along(other, -1)

    q_got = other_half(jnp.concatenate([q_same[half:], q_core[half:]], axis=0), 0, 1)
    q_own = jnp.concatenate([q_same[:half], q_got[:half], q_core[:half], q_got[half:]], axis=0)
    q_up, q_down = queries_along(q_own, 1), queries_along(q_own, -1)
    q_far = queries_along(q_own, 2)

    k_far = keys_along(jnp.concatenate([up_same[:patch], up_other[:patch]], axis=0), 1)
    v_far = keys_along(jnp.concatenate([down_same[patch:], down_other[patch:]], axis=0), -1)

    fresh_keys, fresh_values, up_other, down_other, q_up, q_down = lax.optimization_barrier(
        (fresh_keys, fresh_values, up_other, down_other, q_up, q_down)
    )
    got = other_half(outgoing_fresh(head_table, fresh_keys[0], fresh_values[0]), 0, 1)
    blocks = [same, other, up_same, up_other, down_same, down_other, k_far, v_far]
    o_far = attention(remote_kernel, q_far, blocks)
    o_up = attention(remote_kernel, q_up, blocks)
    o_down = attention(remote_kernel, q_down, blocks)
    far, up, down = queries_along(o_far, 2), queries_along(o_up, -1), queries_along(o_down, 1)
    got, _, _, _ = lax.optimization_barrier((got, o_far, o_up, o_down))
    f_same, f_other = fresh_by_core(table, fresh_keys[0], fresh_values[0], got)
    f_other = other_core(f_other)
    q_own, far, down = lax.optimization_barrier((q_own, far, down))
    o_own = attention(own_kernel, q_own, blocks + [f_same, f_other])
    parts = (o_own, far, up, down)
    theirs = other_core(combine(parts, patch))
    mine = combine(parts, 0)
    pieces = []
    for start, width in ((0, 1536), (1536, out_weight.shape[2] - 1536)):
        first, second = project(core_table, mine, theirs, out_weight[0], out_gate, start, width)
        pieces.append((onward_to(first, 0), onward_to(second, 1)))
    branch = jnp.concatenate(
        [(first.astype(F32) + second.astype(F32)).astype(BF) for first, second in pieces], axis=1
    )
    new_keys, new_values = new_in_order(table, fresh_keys[0], fresh_values[0], got)
    return (new_keys[None], new_values[None], branch[None])


def solution(mesh):
    in_specs = (
        P("pipe", ("patch", "head"), None),
        P("pipe", ("patch", "head"), None),
        P("pipe", ("patch", "head"), None),
        P("pipe", "patch", "head"),
        P("pipe", "patch", "head"),
        P("pipe", "head", None),
        P("pipe", None),
    )
    out_specs = (
        P("pipe", "patch", "head"),
        P("pipe", "patch", "head"),
        P("pipe", ("patch", "head"), None),
    )
    return jax.shard_map(
        per_device, mesh=mesh, in_specs=in_specs, out_specs=out_specs, check_vma=False
    )
```
